32 devices in a mesh: groups: 2 (over y), replica: 4 (over x, core), mp: 4 (over z).
Axes of the slice: x: 2, y: 2, z: 4, core: 2. Of those that a mesh axis runs over, the one named last changes fastest.
Arguments:
- tokens: bfloat16 [8192, 8192], P(('groups', 'replica'), 'mp'), parts along dimension 0, may hold values from -6 to 6
- token_adapter_index: int32 [8192], P(('groups', 'replica')), parts along dimension 0, may hold values from 0 to 31, as said below
- key_value_weight: bfloat16 [8192, 2048], P(None, 'mp'), may hold values from -0.0625 to 0.0625
- adapter_down_weight: bfloat16 [32, 64, 8192], P('replica', None, 'mp'), may hold values from -0.0625 to 0.0625
- adapter_up_weight: bfloat16 [32, 64, 2048], P('replica', None, 'mp'), may hold values from -0.75 to 0.75
Outputs:
- kv_out: bfloat16 [8192, 2048], P(('groups', 'replica'), 'mp'), parts along dimension 0
The draws below stay inside these ranges and needn't reach their ends.
There are 2 independent parts, one for each index of `groups`. The reference program is written for one: setup_inputs(seed, part) draws one part's arguments, and reference() takes and returns one part's arrays. A program takes and returns all parts, laid end to end along the dimension named above; an argument that names none is the same for every part. Nothing has to cross between parts.
Inputs may be any that keep to these rules, and one draw needn't show every extreme that they name: `token_adapter_index`: adapter a is held by index a // 8 of replica. Among the 1024 tokens of one index of replica no adapter id appears more than 32 times, and one adapter id appears exactly 32 times in the tokens of every index of replica. Among them at most 256 have adapters held by one index of replica, and exactly 256 do for one index of replica in the tokens of every index of replica.
All inputs are finite; a program needn't handle non-finite values.
Results may differ from the reference program's by a relative error of at most 0.005.
Values may be sent and summed in bfloat16 or wider, within the bound.
A program may use at most 128 MiB of HBM per device.

```python
import jax
import jax.numpy as jnp
from jax import lax

MODEL_WIDTH = 8192
KEY_VALUE_WIDTH = 2048
ADAPTER_RANK = 64
MOST = 32
ADP_DEV = 8
TOK_DEV = 1024
ADAPTER_TOTAL = 32
TOKENS = 4096
OWN_MOST = 256
N_REPLICA = 4


def draw_token_adapter_index(key, part):
    key = jax.random.fold_in(key, 7)
    favored_key, level_key, block_key = jax.random.split(key, 3)
    slots_all = ADAPTER_TOTAL * MOST
    owner_slots = ADP_DEV * MOST
    favored = jax.random.randint(favored_key, (), 0, ADAPTER_TOTAL)
    labels = jnp.arange(ADAPTER_TOTAL, dtype=jnp.int32)
    levels = jax.random.randint(level_key, (ADAPTER_TOTAL,), 0, 4)
    levels = jnp.where(labels // ADP_DEV == favored // ADP_DEV, 4, levels)
    levels = jnp.where(labels == favored, 5, levels)
    slot_owner = jnp.arange(slots_all, dtype=jnp.int32) // MOST
    slot_order = jnp.arange(slots_all, dtype=jnp.int32)

    def one_block(each_key):
        jitter_key, shuffle_key = jax.random.split(each_key)
        jitter = jax.random.randint(jitter_key, (slots_all,), 0, 1024)
        scores = (levels[slot_owner] * 1024 + jitter) * slots_all + slot_order
        grouped = scores.reshape(N_REPLICA, owner_slots)
        order_in = jnp.argsort(-grouped, axis=1, stable=True).astype(jnp.int32)
        rank_in = jnp.argsort(order_in, axis=1, stable=True).astype(jnp.int32)
        capped = jnp.where(rank_in < OWN_MOST, grouped, -1 - slot_order.reshape(N_REPLICA, owner_slots))
        chosen = lax.top_k(capped.reshape(slots_all), TOK_DEV)[1]
        selected_rows = (chosen // MOST).astype(jnp.int32)
        return jax.random.permutation(shuffle_key, selected_rows)
    blocks = jax.vmap(one_block)(jax.random.split(block_key, N_REPLICA))
    return blocks.reshape(TOKENS).astype(jnp.int32)


def block_levels(rng, dims, shards, low, largest):
    def one(dim, parts):
        steps = jax.random.uniform(jax.random.fold_in(jax.random.fold_in(rng, 6), dim), (parts,), jnp.float32, low / len(shards), largest / len(shards))
        return jnp.repeat(jnp.exp(steps), dims[dim] // parts).reshape((-1,) + (1,) * (len(dims) - dim - 1))

    factor_of = one(*shards[0])
    for cut in shards[1:]:
        factor_of = factor_of * one(*cut)
    return factor_of


def noise(rng, extent, spread, bound, shards=(), kind=jnp.bfloat16):
    entries = spread * jax.random.normal(rng, extent, jnp.float32)
    if shards:
        entries = entries * block_levels(rng, extent, shards, -0.22, 0.18)
    return jnp.clip(entries, -bound, bound).astype(kind)


def setup_inputs(seed: int = 0, part: int = 0) -> dict:
    arg_keys = jax.random.split(jax.random.key(seed), 6)
    part_splits = jax.random.split(jax.random.fold_in(arg_keys[5], part), 6)
    return {
        "tokens": noise(part_splits[0], (TOKENS, MODEL_WIDTH), 1.0, 6.0, ((0, 4), (1, 4))),
        "token_adapter_index": draw_token_adapter_index(jax.random.fold_in(jax.random.fold_in(arg_keys[5], part), 71), part),
        "key_value_weight": noise(arg_keys[2], (MODEL_WIDTH, KEY_VALUE_WIDTH), MODEL_WIDTH ** -0.5, 0.0625, ((1, 4),)),
        "adapter_down_weight": noise(arg_keys[3], (ADAPTER_TOTAL, ADAPTER_RANK, MODEL_WIDTH), MODEL_WIDTH ** -0.5, 0.0625, ((0, 4), (2, 4))),
        "adapter_up_weight": noise(arg_keys[4], (ADAPTER_TOTAL, ADAPTER_RANK, KEY_VALUE_WIDTH), ADAPTER_RANK ** -0.5, 0.75, ((0, 4), (2, 4))),
    }


def reference(tokens, token_adapter_index, key_value_weight, adapter_down_weight, adapter_up_weight):
    base_out = jnp.dot(tokens, key_value_weight, preferred_element_type=jnp.float32)
    count_all = tokens.shape[0]
    capacity = MOST * N_REPLICA
    ordering = jnp.argsort(token_adapter_index, stable=True).astype(jnp.int32)
    sorted_ids = token_adapter_index[ordering]
    firsts = jnp.searchsorted(sorted_ids, jnp.arange(ADAPTER_TOTAL, dtype=jnp.int32)).astype(jnp.int32)

    def per_adapter(carried, adapter_choice):
        position = firsts[adapter_choice] + jnp.arange(capacity, dtype=jnp.int32)
        clipped = jnp.minimum(position, count_all - 1).astype(jnp.int32)
        member = (position < count_all) & (sorted_ids[clipped] == adapter_choice)
        row_ids = ordering[clipped]
        selected_rows = tokens[row_ids]
        reduced_input = jnp.dot(selected_rows, adapter_down_weight[adapter_choice].T, preferred_element_type=jnp.float32).astype(jnp.bfloat16)
        delta_columns = jnp.dot(reduced_input, adapter_up_weight[adapter_choice], preferred_element_type=jnp.float32).astype(jnp.bfloat16)
        target = jnp.where(member, row_ids, count_all).astype(jnp.int32)
        carried = carried.at[target].set(delta_columns, mode="drop")
        return carried, None

    start_delta = jnp.zeros((count_all, KEY_VALUE_WIDTH), jnp.bfloat16)
    delta_full, unused = lax.scan(per_adapter, start_delta, jnp.arange(ADAPTER_TOTAL, dtype=jnp.int32))
    return (base_out + delta_full.astype(jnp.float32)).astype(jnp.bfloat16)
```

```python
import functools

import jax
import jax.numpy as jnp
from jax import lax
from jax.experimental import pallas as pl
from jax.experimental.pallas import tpu as pltpu
from jax.sharding import PartitionSpec as P

BF16 = jnp.bfloat16
F32 = jnp.float32
MESH = pl.DeviceIdType.MESH


def kernel(
    G, R, Z, CH,
    tok_hbm, idx_ref, w_hbm, down_hbm, up_hbm, out_ref,
    tok, wbuf, dbuf, from_left, from_right, sendbuf, low, lowin, base,
    loc_sem, wz_s, wz_r, wp_s, wp_r, ws_s, ws_r,
    rl_s, rl_r, rr_s, rr_r,
    d0_s, d0_r, d1_s, d1_r, d2_s, d2_r, d3_s, d3_r,
    lo_s, lo_r,
):
    T, F = tok.shape
    N = w_hbm.shape[1]
    AR = down_hbm.shape[0]
    X = R // 2
    C = G * X
    FP = F // (G * R)
    HALF = AR // G
    M = T // CH

    g = lax.axis_index("groups")
    r = lax.axis_index("replica")
    z = lax.axis_index("mp")
    x = r // 2
    c = r % 2
    p = g * R + r
    q = g * X + x
    sib = (g, x * 2 + 1 - c, z)

    def chip(k):
        qq = lax.rem(q + k, C)
        return qq, (qq // X, (qq % X) * 2 + c, z)

    barrier = pltpu.get_barrier_semaphore()
    for k in range(1, Z):
        pl.semaphore_signal(barrier, inc=1, device_id=(g, r, lax.rem(z + k, Z)), device_id_type=MESH)
    for k in range(1, C):
        pl.semaphore_signal(barrier, inc=1, device_id=chip(k)[1], device_id_type=MESH)
    pl.semaphore_signal(barrier, inc=1, device_id=sib, device_id_type=MESH)

    own_d = pl.ds(pl.multiple_of(r * AR, AR), AR)
    cp_tok = pltpu.make_async_copy(tok_hbm, tok, loc_sem.at[0])
    cp_w = pltpu.make_async_copy(
        w_hbm.at[pl.ds(pl.multiple_of(z * F, F), F), :], wbuf.at[z], loc_sem.at[1])
    cp_d = pltpu.make_async_copy(down_hbm, dbuf.at[own_d, pl.ds(0, F)], loc_sem.at[2])
    cp_u = pltpu.make_async_copy(up_hbm, dbuf.at[own_d, pl.ds(F, N)], loc_sem.at[3])
    cp_tok.start()
    cp_d.start()
    cp_u.start()
    cp_w.start()
    pl.semaphore_wait(barrier, (Z - 1) + (C - 1) + 1)

    def remote(src, dst, s, rs, dev):
        return pltpu.make_async_remote_copy(
            src_ref=src, dst_ref=dst, send_sem=s, recv_sem=rs, device_id=dev, device_id_type=MESH)

    def wrows(gg, rr):
        return pl.ds(pl.multiple_of((gg * R + rr) * FP, FP), FP)

    def wz(to):
        return remote(
            w_hbm.at[pl.ds(pl.multiple_of(to * F + p * FP, FP), FP), :],
            wbuf.at[z, wrows(g, r), :], wz_s.at[to], wz_r.at[z], (g, r, to))

    def wz_in(b):
        ref = wbuf.at[b, wrows(g, r), :]
        return remote(ref, ref, wz_s.at[b], wz_r.at[b], (g, r, b))

    def wp(b, k):
        qq, dev = chip(k)
        ref = wbuf.at[b, wrows(g, r), :]
        return remote(ref, ref, wp_s.at[b, k], wp_r.at[b, q], dev)

    def wp_in(b, k):
        qq, dev = chip(k)
        ref = wbuf.at[b, wrows(qq // X, (qq % X) * 2 + c), :]
        return remote(ref, ref, wp_s.at[b, k], wp_r.at[b, qq], dev)

    def ws(b, k):
        qq, dev = chip(k)
        ref = wbuf.at[b, wrows(qq // X, (qq % X) * 2 + c), :]
        return remote(ref, ref, ws_s.at[b, qq], ws_r.at[b, qq], sib)

    def ws_in(b, k):
        qq, dev = chip(k)
        ref = wbuf.at[b, wrows(qq // X, (qq % X) * 2 + 1 - c), :]
        return remote(ref, ref, ws_s.at[b, qq], ws_r.at[b, qq], sib)

    def gather_w(b):
        wz_in(b).wait_recv()
        for k in range(1, C):
            wp(b, k).start()
        ws(b, 0).start()
        for k in range(1, C):
            wp_in(b, k).wait_recv()
            ws(b, k).start()
        for k in range(C):
            ws_in(b, k).wait_recv()

    for s in range(Z - 1):
        @pl.when(Z - 1 - s > z)
        def _(s=s):
            wz(Z - 1 - s).start()

        @pl.when(s < z)
        def _(s=s):
            wz(s).start()

    def drows(rr, h):
        return pl.ds(pl.multiple_of(rr * AR + h * HALF, HALF), HALF)

    def d0():
        ref = dbuf.at[own_d, :]
        return remote(ref, ref, d0_s, d0_r, sib)

    def d0_in():
        ref = dbuf.at[pl.ds(pl.multiple_of((x * 2 + 1 - c) * AR, AR), AR), :]
        return remote(ref, ref, d0_s, d0_r, sib)

    def d1(k):
        ref = dbuf.at[drows(r, g), :]
        return remote(ref, ref, d1_s.at[k], d1_r.at[x], (g, lax.rem(x + k, X) * 2 + c, z))

    def xk(k):
        return lax.rem(x + k, X)

    def d1_in(k):
        ref = dbuf.at[drows(xk(k) * 2 + c, g), :]
        return remote(ref, ref, d1_s.at[k], d1_r.at[xk(k)], (g, xk(k) * 2 + c, z))

    def d2(k, j):
        ref = dbuf.at[drows(xk(k) * 2 + c, g), :]
        return remote(ref, ref, d2_s.at[k, j], d2_r.at[xk(k), g], (lax.rem(g + j, G), r, z))

    def d2_in(k, j):
        gg = lax.rem(g + j, G)
        ref = dbuf.at[drows(xk(k) * 2 + c, gg), :]
        return remote(ref, ref, d2_s.at[k, j], d2_r.at[xk(k), gg], (gg, r, z))

    def d3(k, h):
        ref = dbuf.at[drows(xk(k) * 2 + c, h), :]
        return remote(ref, ref, d3_s.at[xk(k), h], d3_r.at[xk(k), h], sib)

    def d3_in(k, h):
        ref = dbuf.at[drows(xk(k) * 2 + 1 - c, h), :]
        return remote(ref, ref, d3_s.at[xk(k), h], d3_r.at[xk(k), h], sib)

    lane_half = lax.broadcasted_iota(jnp.int32, (CH, 128), 1) // 64

    def rows(m):
        return pl.ds(pl.multiple_of(m * CH, CH), CH)

    low[...] = jnp.zeros_like(low)

    def shrink(rr):
        src = pl.ds(pl.multiple_of(rr * AR, AR), AR)

        @pl.loop(0, M)
        def _(m):
            y = lax.dot_general(
                tok[rows(m), :], dbuf[src, pl.ds(0, F)], (((1,), (1,)), ((), ())),
                preferred_element_type=F32)
            mine = idx_ref[rows(m), :] - rr * (AR // 64) - lane_half
            part = low[rows(m), :]
            for t in range(AR // 128):
                part += jnp.where(mine == 2 * t, y[:, t * 128:(t + 1) * 128], 0.0)
            low[rows(m), :] = part

    cp_tok.wait()
    cp_d.wait()
    cp_u.wait()
    d0().start()
    shrink(r)

    def to_right(b, m):
        return remote(sendbuf.at[b, rows(m), :], from_left.at[b, rows(m), :],
                      rl_s.at[b, m], rl_r.at[b, m], (g, r, lax.rem(z + 1, Z)))

    def to_left(b, m):
        return remote(sendbuf.at[b, rows(m), :], from_right.at[b, rows(m), :],
                      rr_s.at[b, m], rr_r.at[b, m], (g, r, lax.rem(z + Z - 1, Z)))

    def chain(b, landed, make, first):
        @pl.loop(0, M)
        def _(m):
            y = jnp.dot(tok[rows(m), :], wbuf[b], preferred_element_type=F32)

            @pl.when(first)
            def _():
                sendbuf[b, rows(m), :] = y.astype(BF16)

            @pl.when(jnp.logical_not(first))
            def _():
                make(b, m).wait_recv()
                sendbuf[b, rows(m), :] = (y + landed[b, rows(m), :].astype(F32)).astype(BF16)

            make(b, m).start()

    for s in range(Z - 1):
        @pl.when(Z - 1 - s > z)
        def _(b=Z - 1 - s):
            gather_w(b)
            chain(b, from_left, to_right, z == 0)

        @pl.when(s < z)
        def _(b=s):
            gather_w(b)
            chain(b, from_right, to_left, z == Z - 1)

        if s == 0:
            for k in range(1, X):
                d1(k).start()

    for k in range(1, X):
        d1_in(k).wait_recv()
        for j in range(1, G):
            d2(k, j).start()
        d3(k, g).start()
    d0_in().wait_recv()
    shrink(x * 2 + 1 - c)
    for k in range(1, X):
        for j in range(1, G):
            d2_in(k, j).wait_recv()
            d3(k, lax.rem(g + j, G)).start()
        shrink(xk(k) * 2 + c)
    for k in range(1, X):
        for h in range(G):
            d3_in(k, h).wait_recv()
        shrink(xk(k) * 2 + 1 - c)

    H = T // 2
    left_lanes = lax.broadcasted_iota(jnp.int32, (H, 128), 1) < 64
    both = low[...]
    both = both + pltpu.roll(both, 64, 1)
    packed = jnp.where(left_lanes, both[:H], both[H:])
    lowin[z] = packed.astype(BF16)

    def lo(k):
        return remote(lowin.at[z], lowin.at[z], lo_s.at[k], lo_r.at[z], (g, r, lax.rem(z + k, Z)))

    def lo_in(k):
        zz = lax.rem(z + k, Z)
        return remote(lowin.at[zz], lowin.at[zz], lo_s.at[k], lo_r.at[zz], (g, r, zz))

    for k in range(1, Z):
        lo(k).start()

    cp_w.wait()

    @pl.loop(0, M)
    def _(m):
        base[rows(m), :] = jnp.dot(tok[rows(m), :], wbuf[z], preferred_element_type=F32)

    total = packed
    for k in range(1, Z):
        lo_in(k).wait_recv()
        total = total + lowin[lax.rem(z + k, Z)].astype(F32)
    total = total.astype(BF16).astype(F32)
    other = pltpu.roll(total, 64, 1)
    low[pl.ds(0, H), :] = jnp.where(left_lanes, total, other)
    low[pl.ds(H, H), :] = jnp.where(left_lanes, other, total)

    @pl.loop(0, M)
    def _(m):
        ss = low[rows(m), :]
        who = idx_ref[rows(m), :] - lane_half

        def add(rr, acc):
            lhs = jnp.concatenate(
                [jnp.where(who == rr * (AR // 64) + 2 * t, ss, 0.0).astype(BF16) for t in range(AR // 128)],
                axis=1)
            return acc + jnp.dot(
                lhs, dbuf[pl.ds(pl.multiple_of(rr * AR, AR), AR), pl.ds(F, N)],
                preferred_element_type=F32)

        delta = lax.fori_loop(0, R, add, jnp.zeros((CH, N), F32))
        base[rows(m), :] = base[rows(m), :] + delta.astype(BF16).astype(F32)

    @pl.when(z > 0)
    def _():
        @pl.loop(0, M)
        def _(m):
            to_right(z, m).wait_recv()
            base[rows(m), :] = base[rows(m), :] + from_left[z, rows(m), :].astype(F32)

    @pl.when(z < Z - 1)
    def _():
        @pl.loop(0, M)
        def _(m):
            to_left(z, m).wait_recv()
            base[rows(m), :] = base[rows(m), :] + from_right[z, rows(m), :].astype(F32)

    out_ref[...] = base[...].astype(BF16)

    for b in range(Z):
        @pl.when(b != z)
        def _(b=b):
            wz(b).wait_send()
            for k in range(1, C):
                wp(b, k).wait_send()
            for k in range(C):
                ws(b, k).wait_send()

        @pl.when(b > z)
        def _(b=b):
            @pl.loop(0, M)
            def _(m):
                to_right(b, m).wait_send()

        @pl.when(b < z)
        def _(b=b):
            @pl.loop(0, M)
            def _(m):
                to_left(b, m).wait_send()
    d0().wait_send()
    for k in range(1, X):
        d1(k).wait_send()
        for j in range(1, G):
            d2(k, j).wait_send()
        for h in range(G):
            d3(k, h).wait_send()
    for k in range(1, Z):
        lo(k).wait_send()


def shards(G, R, Z, tokens, token_adapter_index, key_value_weight, adapter_down_weight, adapter_up_weight):
    T, F = tokens.shape
    N = key_value_weight.shape[1]
    A, K, _ = adapter_down_weight.shape
    AR = A * K
    CH = min(256, T)
    M = T // CH
    X = R // 2
    C = G * X
    idx = jnp.broadcast_to(token_adapter_index[:, None], (T, 128))
    dma = pltpu.SemaphoreType.DMA
    any_spec = pl.BlockSpec(memory_space=pl.ANY)
    vmem_spec = pl.BlockSpec(memory_space=pltpu.VMEM)
    return pl.pallas_call(
        functools.partial(kernel, G, R, Z, CH),
        out_shape=jax.ShapeDtypeStruct((T, N), BF16),
        in_specs=[any_spec, vmem_spec, any_spec, any_spec, any_spec],
        out_specs=vmem_spec,
        scratch_shapes=[
            pltpu.VMEM((T, F), BF16),
            pltpu.VMEM((Z, F, N), BF16),
            pltpu.VMEM((R * AR, F + N), BF16),
            pltpu.VMEM((Z, T, N), BF16),
            pltpu.VMEM((Z, T, N), BF16),
            pltpu.VMEM((Z, T, N), BF16),
            pltpu.VMEM((T, 128), F32),
            pltpu.VMEM((Z, T // 2, 128), BF16),
            pltpu.VMEM((T, N), F32),
            dma((4,)), dma((Z,)), dma((Z,)), dma((Z, C)), dma((Z, C)), dma((Z, C)), dma((Z, C)),
            dma((Z, M)), dma((Z, M)), dma((Z, M)), dma((Z, M)),
            dma, dma, dma((X,)), dma((X,)), dma((X, G)), dma((X, G)), dma((X, G)), dma((X, G)),
            dma((Z,)), dma((Z,)),
        ],
        compiler_params=pltpu.CompilerParams(
            collective_id=0, has_side_effects=True, vmem_limit_bytes=58 * 1024 * 1024),
    )(tokens, idx, key_value_weight, adapter_down_weight.reshape(AR, F), adapter_up_weight.reshape(AR, N))


def solution(mesh):
    G, R, Z = (mesh.shape[a] for a in ("groups", "replica", "mp"))
    return jax.shard_map(
        functools.partial(shards, G, R, Z),
        mesh=mesh,
        in_specs=(
            P(("groups", "replica"), "mp"),
            P(("groups", "replica")),
            P(None, "mp"),
            P("replica", None, "mp"),
            P("replica", None, "mp"),
        ),
        out_specs=P(("groups", "replica"), "mp"),
        check_vma=False,
    )
```

```python
import functools

import jax
import jax.numpy as jnp
from jax import lax
from jax.experimental import pallas as pl
from jax.experimental.pallas import tpu as pltpu
from jax.sharding import PartitionSpec as P

BF16 = jnp.bfloat16
F32 = jnp.float32
MESH = pl.DeviceIdType.MESH


def kernel(
    G, R, Z, CH,
    tok_hbm, idx_ref, w_hbm, down_hbm, up_hbm, out_ref,
    tok, wbuf, dbuf, from_left, from_right, sendbuf, low, lowin, base,
    loc_sem, wz_s, wz_r, wp_s, wp_r, wc_s, wc_r, ws_s, ws_r,
    rl_s, rl_r, rr_s, rr_r,
    d0_s, d0_r, d1_s, d1_r, d2_s, d2_r, d3_s, d3_r,
    lo_s, lo_r,
):
    T, F = tok.shape
    N = w_hbm.shape[1]
    AR = down_hbm.shape[0]
    X = R // 2
    C = G * X
    FP = F // (G * R)
    HALF = AR // G
    M = T // CH

    g = lax.axis_index("groups")
    r = lax.axis_index("replica")
    z = lax.axis_index("mp")
    x = r // 2
    c = r % 2
    p = g * R + r
    q = g * X + x
    sib = (g, x * 2 + 1 - c, z)

    def chip(k):
        gg, xx = lax.rem(g + k // X, G), lax.rem(x + k % X, X)
        return gg * X + xx, (gg, xx * 2 + c, z)

    barrier = pltpu.get_barrier_semaphore()
    for k in range(1, Z):
        pl.semaphore_signal(barrier, inc=1, device_id=(g, r, lax.rem(z + k, Z)), device_id_type=MESH)
    for k in range(1, C):
        pl.semaphore_signal(barrier, inc=1, device_id=chip(k)[1], device_id_type=MESH)
    pl.semaphore_signal(barrier, inc=1, device_id=sib, device_id_type=MESH)

    own_d = pl.ds(pl.multiple_of(r * AR, AR), AR)
    cp_tok = pltpu.make_async_copy(tok_hbm, tok, loc_sem.at[0])
    cp_w = pltpu.make_async_copy(
        w_hbm.at[pl.ds(pl.multiple_of(z * F, F), F), :], wbuf.at[z], loc_sem.at[1])
    cp_d = pltpu.make_async_copy(down_hbm, dbuf.at[own_d, pl.ds(0, F)], loc_sem.at[2])
    cp_u = pltpu.make_async_copy(up_hbm, dbuf.at[own_d, pl.ds(F, N)], loc_sem.at[3])
    cp_tok.start()
    cp_d.start()
    cp_u.start()
    cp_w.start()
    pl.semaphore_wait(barrier, (Z - 1) + (C - 1) + 1)

    def remote(src, dst, s, rs, dev):
        return pltpu.make_async_remote_copy(
            src_ref=src, dst_ref=dst, send_sem=s, recv_sem=rs, device_id=dev, device_id_type=MESH)

    def wrows(gg, rr):
        return pl.ds(pl.multiple_of((gg * R + rr) * FP, FP), FP)

    def wz(to):
        return remote(
            w_hbm.at[pl.ds(pl.multiple_of(to * F + p * FP, FP), FP), :],
            wbuf.at[z, wrows(g, r), :], wz_s.at[to], wz_r.at[z], (g, r, to))

    def wz_in(b):
        ref = wbuf.at[b, wrows(g, r), :]
        return remote(ref, ref, wz_s.at[b], wz_r.at[b], (g, r, b))

    def wp(b, n):
        ref = wbuf.at[b, wrows(g, r), :]
        return remote(ref, ref, wp_s.at[b, n], wp_r.at[b, q], line(n)[1])

    def line(n):
        if n < X - 1:
            gg, xx = g, lax.rem(x + n + 1, X)
        else:
            gg, xx = lax.rem(g + n - X + 2, G), x
        return gg * X + xx, (gg, xx * 2 + c, z)

    def wp_in(b, n):
        qq, dev = line(n)
        ref = wbuf.at[b, wrows(qq // X, (qq % X) * 2 + c), :]
        return remote(ref, ref, wp_s.at[b, n], wp_r.at[b, qq], dev)

    def half(gg, xx, h):
        return pl.ds(pl.multiple_of((gg * R + xx * 2 + c) * FP + h * (FP // 2), FP // 2), FP // 2)

    def wc(b, i, j, h):
        gg, xx = lax.rem(g + j, G), lax.rem(x + i, X)
        if h == 0:
            ref, src, dev = wbuf.at[b, half(g, xx, 0), :], g * X + xx, (gg, r, z)
        else:
            ref, src, dev = wbuf.at[b, half(gg, x, 1), :], gg * X + x, (g, xx * 2 + c, z)
        return remote(ref, ref, wc_s.at[b, (i * G + j) * 2 + h], wc_r.at[b, src * 2 + h], dev)

    def wc_in(b, i, j, h):
        gg, xx = lax.rem(g + j, G), lax.rem(x + i, X)
        ref = wbuf.at[b, half(gg, xx, h), :]
        return remote(ref, ref, wc_s.at[b, (i * G + j) * 2 + h], wc_r.at[b, (gg * X + xx) * 2 + h], (gg, r, z))

    def ws(b, k):
        qq, dev = chip(k)
        ref = wbuf.at[b, wrows(qq // X, (qq % X) * 2 + c), :]
        return remote(ref, ref, ws_s.at[b, qq], ws_r.at[b, qq], sib)

    def ws_in(b, k):
        qq, dev = chip(k)
        ref = wbuf.at[b, wrows(qq // X, (qq % X) * 2 + 1 - c), :]
        return remote(ref, ref, ws_s.at[b, qq], ws_r.at[b, qq], sib)

    LINES = X - 1 + G - 1

    def gather_a(b):
        wz_in(b).wait_recv()
        for n in range(LINES):
            wp(b, n).start()
        ws(b, 0).start()

    def gather_b(b):
        for n in range(LINES):
            wp_in(b, n).wait_recv()
            if n < X - 1:
                for j in range(1, G):
                    wc(b, n + 1, j, 0).start()
            else:
                for i in range(1, X):
                    wc(b, i, n - X + 2, 1).start()
        for k in range(1, X):
            ws(b, k).start()
        for j in range(1, G):
            ws(b, X * j).start()

    def gather_corner(b):
        for i in range(1, X):
            for j in range(1, G):
                wc_in(b, i, j, 0).wait_recv()
                wc_in(b, i, j, 1).wait_recv()
                ws(b, X * j + i).start()

    def gather_c(b):
        for k in range(C):
            ws_in(b, k).wait_recv()

    def blocks(s, do_right, do_left):
        @pl.when(Z - 1 - s > z)
        def _():
            do_right(Z - 1 - s)

        @pl.when(s < z)
        def _():
            do_left(s)

    for s in range(Z - 1):
        @pl.when(Z - 1 - s > z)
        def _(s=s):
            wz(Z - 1 - s).start()

        @pl.when(s < z)
        def _(s=s):
            wz(s).start()

    def drows(rr, h):
        return pl.ds(pl.multiple_of(rr * AR + h * HALF, HALF), HALF)

    def d0():
        ref = dbuf.at[own_d, :]
        return remote(ref, ref, d0_s, d0_r, sib)

    def d0_in():
        ref = dbuf.at[pl.ds(pl.multiple_of((x * 2 + 1 - c) * AR, AR), AR), :]
        return remote(ref, ref, d0_s, d0_r, sib)

    def d1(k):
        ref = dbuf.at[drows(r, g), :]
        return remote(ref, ref, d1_s.at[k], d1_r.at[x], (g, lax.rem(x + k, X) * 2 + c, z))

    def xk(k):
        return lax.rem(x + k, X)

    def d1_in(k):
        ref = dbuf.at[drows(xk(k) * 2 + c, g), :]
        return remote(ref, ref, d1_s.at[k], d1_r.at[xk(k)], (g, xk(k) * 2 + c, z))

    def d2(k, j):
        ref = dbuf.at[drows(xk(k) * 2 + c, g), :]
        return remote(ref, ref, d2_s.at[k, j], d2_r.at[xk(k), g], (lax.rem(g + j, G), r, z))

    def d2_in(k, j):
        gg = lax.rem(g + j, G)
        ref = dbuf.at[drows(xk(k) * 2 + c, gg), :]
        return remote(ref, ref, d2_s.at[k, j], d2_r.at[xk(k), gg], (gg, r, z))

    def d3(k, h):
        ref = dbuf.at[drows(xk(k) * 2 + c, h), :]
        return remote(ref, ref, d3_s.at[xk(k), h], d3_r.at[xk(k), h], sib)

    def d3_in(k, h):
        ref = dbuf.at[drows(xk(k) * 2 + 1 - c, h), :]
        return remote(ref, ref, d3_s.at[xk(k), h], d3_r.at[xk(k), h], sib)

    lane_half = lax.broadcasted_iota(jnp.int32, (CH, 128), 1) // 64
    BIG = min(512, T)
    lane_big = lax.broadcasted_iota(jnp.int32, (BIG, 128), 1) // 64

    def big(m):
        return pl.ds(pl.multiple_of(m * BIG, BIG), BIG)

    def rows(m):
        return pl.ds(pl.multiple_of(m * CH, CH), CH)

    low[...] = jnp.zeros_like(low)

    def shrink(rr):
        src = pl.ds(pl.multiple_of(rr * AR, AR), AR)

        @pl.loop(0, T // BIG)
        def _(m):
            y = lax.dot_general(
                tok[big(m), :], dbuf[src, pl.ds(0, F)], (((1,), (1,)), ((), ())),
                preferred_element_type=F32)
            mine = idx_ref[big(m), :] - rr * (AR // 64) - lane_big
            part = low[big(m), :]
            for t in range(AR // 128):
                part += jnp.where(mine == 2 * t, y[:, t * 128:(t + 1) * 128], 0.0)
            low[big(m), :] = part

    cp_tok.wait()
    cp_d.wait()
    cp_u.wait()
    for k in range(1, X):
        d1(k).start()
    d0().start()
    shrink(r)
    cp_w.wait()

    @pl.loop(0, T // BIG)
    def _(m):
        base[big(m), :] = jnp.dot(tok[big(m), :], wbuf[z], preferred_element_type=F32)

    def to_right(b, m):
        return remote(sendbuf.at[b, rows(m), :], from_left.at[b, rows(m), :],
                      rl_s.at[b, m], rl_r.at[b, m], (g, r, lax.rem(z + 1, Z)))

    def to_left(b, m):
        return remote(sendbuf.at[b, rows(m), :], from_right.at[b, rows(m), :],
                      rr_s.at[b, m], rr_r.at[b, m], (g, r, lax.rem(z + Z - 1, Z)))

    def chain_first(b, make):
        @pl.loop(0, M)
        def _(m):
            sendbuf[b, rows(m), :] = jnp.dot(
                tok[rows(m), :], wbuf[b], preferred_element_type=F32).astype(BF16)
            make(b, m).start()

    def chain(b, landed, make):
        @pl.loop(0, M)
        def _(m):
            y = jnp.dot(tok[rows(m), :], wbuf[b], preferred_element_type=F32)
            make(b, m).wait_recv()
            sendbuf[b, rows(m), :] = (y + landed[b, rows(m), :].astype(F32)).astype(BF16)
            make(b, m).start()

    def middle(k):
        right = Z - 1 + z - k

        @pl.when((z > 0) & (right > z) & (right < Z))
        def _():
            chain(right, from_left, to_right)

        left = k - (Z - 1 - z)

        @pl.when((z < Z - 1) & (left >= 0) & (left < z))
        def _():
            chain(left, from_right, to_left)

    def finish_right(b):
        gather_corner(b)
        gather_c(b)

        @pl.when(z == 0)
        def _():
            chain_first(b, to_right)

    def finish_left(b):
        gather_corner(b)
        gather_c(b)

        @pl.when(z == Z - 1)
        def _():
            chain_first(b, to_left)

    blocks(0, gather_a, gather_a)
    for s in range(Z - 1):
        blocks(s, gather_b, gather_b)
        if s + 1 < Z - 1:
            blocks(s + 1, gather_a, gather_a)
        blocks(s, finish_right, finish_left)

    d0_in().wait_recv()
    shrink(x * 2 + 1 - c)
    for k in range(1, X):
        d1_in(k).wait_recv()
        for j in range(1, G):
            d2(k, j).start()
        d3(k, g).start()
    if Z > 2:
        middle(1)
    for k in range(1, X):
        for j in range(1, G):
            d2_in(k, j).wait_recv()
            d3(k, lax.rem(g + j, G)).start()
        shrink(xk(k) * 2 + c)
    for k in range(1, X):
        for h in range(G):
            d3_in(k, h).wait_recv()
        shrink(xk(k) * 2 + 1 - c)

    H = T // 2
    left_lanes = lax.broadcasted_iota(jnp.int32, (H, 128), 1) < 64
    both = low[...]
    both = both + pltpu.roll(both, 64, 1)
    packed = jnp.where(left_lanes, both[:H], both[H:])
    lowin[z] = packed.astype(BF16)

    def lo(k):
        return remote(lowin.at[z], lowin.at[z], lo_s.at[k], lo_r.at[z], (g, r, lax.rem(z + k, Z)))

    def lo_in(k):
        zz = lax.rem(z + k, Z)
        return remote(lowin.at[zz], lowin.at[zz], lo_s.at[k], lo_r.at[zz], (g, r, zz))

    for k in range(1, Z):
        lo(k).start()

    if Z > 2:
        for k in range(2, Z - 1):
            middle(k)

    total = packed
    for k in range(1, Z):
        lo_in(k).wait_recv()
        total = total + lowin[lax.rem(z + k, Z)].astype(F32)
    total = total.astype(BF16).astype(F32)
    other = pltpu.roll(total, 64, 1)
    low[pl.ds(0, H), :] = jnp.where(left_lanes, total, other)
    low[pl.ds(H, H), :] = jnp.where(left_lanes, other, total)

    @pl.loop(0, T // BIG)
    def _(m):
        ss = low[big(m), :]
        who = idx_ref[big(m), :] - lane_big

        def add(rr, acc):
            lhs = jnp.concatenate(
                [jnp.where(who == rr * (AR // 64) + 2 * t, ss, 0.0).astype(BF16) for t in range(AR // 128)],
                axis=1)
            return acc + jnp.dot(
                lhs, dbuf[pl.ds(pl.multiple_of(rr * AR, AR), AR), pl.ds(F, N)],
                preferred_element_type=F32)

        delta = lax.fori_loop(0, R, add, jnp.zeros((BIG, N), F32))
        base[big(m), :] = base[big(m), :] + delta.astype(BF16).astype(F32)

    @pl.when(z > 0)
    def _():
        @pl.loop(0, M)
        def _(m):
            to_right(z, m).wait_recv()
            base[rows(m), :] = base[rows(m), :] + from_left[z, rows(m), :].astype(F32)

    @pl.when(z < Z - 1)
    def _():
        @pl.loop(0, M)
        def _(m):
            to_left(z, m).wait_recv()
            base[rows(m), :] = base[rows(m), :] + from_right[z, rows(m), :].astype(F32)

    out_ref[...] = base[...].astype(BF16)

    for b in range(Z):
        @pl.when(b != z)
        def _(b=b):
            wz(b).wait_send()
            for n in range(LINES):
                wp(b, n).wait_send()
            for i in range(1, X):
                for j in range(1, G):
                    wc(b, i, j, 0).wait_send()
                    wc(b, i, j, 1).wait_send()
            for k in range(C):
                ws(b, k).wait_send()

        @pl.when(b > z)
        def _(b=b):
            @pl.loop(0, M)
            def _(m):
                to_right(b, m).wait_send()

        @pl.when(b < z)
        def _(b=b):
            @pl.loop(0, M)
            def _(m):
                to_left(b, m).wait_send()
    d0().wait_send()
    for k in range(1, X):
        d1(k).wait_send()
        for j in range(1, G):
            d2(k, j).wait_send()
        for h in range(G):
            d3(k, h).wait_send()
    for k in range(1, Z):
        lo(k).wait_send()


def shards(G, R, Z, tokens, token_adapter_index, key_value_weight, adapter_down_weight, adapter_up_weight):
    T, F = tokens.shape
    N = key_value_weight.shape[1]
    A, K, _ = adapter_down_weight.shape
    AR = A * K
    CH = min(256, T)
    M = T // CH
    X = R // 2
    C = G * X
    idx = jnp.broadcast_to(token_adapter_index[:, None], (T, 128))
    dma = pltpu.SemaphoreType.DMA
    any_spec = pl.BlockSpec(memory_space=pl.ANY)
    vmem_spec = pl.BlockSpec(memory_space=pltpu.VMEM)
    return pl.pallas_call(
        functools.partial(kernel, G, R, Z, CH),
        out_shape=jax.ShapeDtypeStruct((T, N), BF16),
        in_specs=[any_spec, vmem_spec, any_spec, any_spec, any_spec],
        out_specs=vmem_spec,
        scratch_shapes=[
            pltpu.VMEM((T, F), BF16),
            pltpu.VMEM((Z, F, N), BF16),
            pltpu.VMEM((R * AR, F + N), BF16),
            pltpu.VMEM((Z, T, N), BF16),
            pltpu.VMEM((Z, T, N), BF16),
            pltpu.VMEM((Z, T, N), BF16),
            pltpu.VMEM((T, 128), F32),
            pltpu.VMEM((Z, T // 2, 128), BF16),
            pltpu.VMEM((T, N), F32),
            dma((4,)), dma((Z,)), dma((Z,)), dma((Z, C)), dma((Z, C)), dma((Z, 2 * C)), dma((Z, 2 * C)), dma((Z, C)), dma((Z, C)),
            dma((Z, M)), dma((Z, M)), dma((Z, M)), dma((Z, M)),
            dma, dma, dma((X,)), dma((X,)), dma((X, G)), dma((X, G)), dma((X, G)), dma((X, G)),
            dma((Z,)), dma((Z,)),
        ],
        compiler_params=pltpu.CompilerParams(
            collective_id=0, has_side_effects=True, vmem_limit_bytes=58 * 1024 * 1024),
    )(tokens, idx, key_value_weight, adapter_down_weight.reshape(AR, F), adapter_up_weight.reshape(AR, N))


def solution(mesh):
    G, R, Z = (mesh.shape[a] for a in ("groups", "replica", "mp"))
    return jax.shard_map(
        functools.partial(shards, G, R, Z),
        mesh=mesh,
        in_specs=(
            P(("groups", "replica"), "mp"),
            P(("groups", "replica")),
            P(None, "mp"),
            P("replica", None, "mp"),
            P("replica", None, "mp"),
        ),
        out_specs=P(("groups", "replica"), "mp"),
        check_vma=False,
    )
```

```python
import functools

import jax
import jax.numpy as jnp
from jax import lax
from jax.experimental import pallas as pl
from jax.experimental.pallas import tpu as pltpu
from jax.sharding import PartitionSpec as P

BF16 = jnp.bfloat16
F32 = jnp.float32
MESH = pl.DeviceIdType.MESH


def kernel(
    G, R, Z, CH,
    tok_hbm, idx_ref, w_hbm, down_hbm, up_hbm, out_ref,
    tok, wbuf, dbuf, from_left, from_right, sendbuf, low, lowin, base,
    loc_sem, wz_s, wz_r, wp_s, wp_r, wc_s, wc_r, ws_s, ws_r,
    rl_s, rl_r, rr_s, rr_r,
    d0_s, d0_r, d1_s, d1_r, d2_s, d2_r, d3_s, d3_r,
    lo_s, lo_r,
):
    T, F = tok.shape
    N = w_hbm.shape[1]
    AR = down_hbm.shape[0]
    X = R // 2
    C = G * X
    FP = F // (G * R)
    HALF = AR // G
    M = T // CH

    g = lax.axis_index("groups")
    r = lax.axis_index("replica")
    z = lax.axis_index("mp")
    x = r // 2
    c = r % 2
    p = g * R + r
    q = g * X + x
    sib = (g, x * 2 + 1 - c, z)

    def chip(k):
        gg, xx = lax.rem(g + k // X, G), lax.rem(x + k % X, X)
        return gg * X + xx, (gg, xx * 2 + c, z)

    barrier = pltpu.get_barrier_semaphore()
    for k in range(1, Z):
        pl.semaphore_signal(barrier, inc=1, device_id=(g, r, lax.rem(z + k, Z)), device_id_type=MESH)
    for k in range(1, C):
        pl.semaphore_signal(barrier, inc=1, device_id=chip(k)[1], device_id_type=MESH)
    pl.semaphore_signal(barrier, inc=1, device_id=sib, device_id_type=MESH)

    own_d = pl.ds(pl.multiple_of(r * AR, AR), AR)
    cp_tok = pltpu.make_async_copy(tok_hbm, tok, loc_sem.at[0])
    cp_w = pltpu.make_async_copy(
        w_hbm.at[pl.ds(pl.multiple_of(z * F, F), F), :], wbuf.at[z], loc_sem.at[1])
    cp_d = pltpu.make_async_copy(down_hbm, dbuf.at[own_d, pl.ds(0, F)], loc_sem.at[2])
    cp_u = pltpu.make_async_copy(up_hbm, dbuf.at[own_d, pl.ds(F, N)], loc_sem.at[3])
    cp_tok.start()
    cp_d.start()
    cp_u.start()
    cp_w.start()
    pl.semaphore_wait(barrier, (Z - 1) + (C - 1) + 1)

    def remote(src, dst, s, rs, dev):
        return pltpu.make_async_remote_copy(
            src_ref=src, dst_ref=dst, send_sem=s, recv_sem=rs, device_id=dev, device_id_type=MESH)

    def wrows(gg, rr):
        return pl.ds(pl.multiple_of((gg * R + rr) * FP, FP), FP)

    def wz(to):
        return remote(
            w_hbm.at[pl.ds(pl.multiple_of(to * F + p * FP, FP), FP), :],
            wbuf.at[z, wrows(g, r), :], wz_s.at[to], wz_r.at[z], (g, r, to))

    def wz_in(b):
        ref = wbuf.at[b, wrows(g, r), :]
        return remote(ref, ref, wz_s.at[b], wz_r.at[b], (g, r, b))

    def wp(b, n):
        ref = wbuf.at[b, wrows(g, r), :]
        return remote(ref, ref, wp_s.at[b, n], wp_r.at[b, q], line(n)[1])

    def line(n):
        if n < X - 1:
            gg, xx = g, lax.rem(x + n + 1, X)
        else:
            gg, xx = lax.rem(g + n - X + 2, G), x
        return gg * X + xx, (gg, xx * 2 + c, z)

    def wp_in(b, n):
        qq, dev = line(n)
        ref = wbuf.at[b, wrows(qq // X, (qq % X) * 2 + c), :]
        return remote(ref, ref, wp_s.at[b, n], wp_r.at[b, qq], dev)

    def half(gg, xx, h):
        return pl.ds(pl.multiple_of((gg * R + xx * 2 + c) * FP + h * (FP // 2), FP // 2), FP // 2)

    def wc(b, i, j, h):
        gg, xx = lax.rem(g + j, G), lax.rem(x + i, X)
        if h == 0:
            ref, src, dev = wbuf.at[b, half(g, xx, 0), :], g * X + xx, (gg, r, z)
        else:
            ref, src, dev = wbuf.at[b, half(gg, x, 1), :], gg * X + x, (g, xx * 2 + c, z)
        return remote(ref, ref, wc_s.at[b, (i * G + j) * 2 + h], wc_r.at[b, src * 2 + h], dev)

    def wc_in(b, i, j, h):
        gg, xx = lax.rem(g + j, G), lax.rem(x + i, X)
        ref = wbuf.at[b, half(gg, xx, h), :]
        return remote(ref, ref, wc_s.at[b, (i * G + j) * 2 + h], wc_r.at[b, (gg * X + xx) * 2 + h], (gg, r, z))

    def ws(b, k):
        qq, dev = chip(k)
        ref = wbuf.at[b, wrows(qq // X, (qq % X) * 2 + c), :]
        return remote(ref, ref, ws_s.at[b, qq], ws_r.at[b, qq], sib)

    def ws_in(b, k):
        qq, dev = chip(k)
        ref = wbuf.at[b, wrows(qq // X, (qq % X) * 2 + 1 - c), :]
        return remote(ref, ref, ws_s.at[b, qq], ws_r.at[b, qq], sib)

    LINES = X - 1 + G - 1

    def gather_a(b):
        wz_in(b).wait_recv()
        for n in range(LINES):
            wp(b, n).start()
        ws(b, 0).start()

    def gather_b(b):
        for n in range(LINES):
            wp_in(b, n).wait_recv()
            if n < X - 1:
                for j in range(1, G):
                    wc(b, n + 1, j, 0).start()
            else:
                for i in range(1, X):
                    wc(b, i, n - X + 2, 1).start()
        for k in range(1, X):
            ws(b, k).start()
        for j in range(1, G):
            ws(b, X * j).start()

    def gather_corner(b):
        for i in range(1, X):
            for j in range(1, G):
                wc_in(b, i, j, 0).wait_recv()
                wc_in(b, i, j, 1).wait_recv()
                ws(b, X * j + i).start()

    def gather_c(b):
        for k in range(C):
            ws_in(b, k).wait_recv()

    def blocks(s, do_right, do_left):
        @pl.when(Z - 1 - s > z)
        def _():
            do_right(Z - 1 - s)

        @pl.when(s < z)
        def _():
            do_left(s)

    for s in range(Z - 1):
        @pl.when(Z - 1 - s > z)
        def _(s=s):
            wz(Z - 1 - s).start()

        @pl.when(s < z)
        def _(s=s):
            wz(s).start()

    def drows(rr, h):
        return pl.ds(pl.multiple_of(rr * AR + h * HALF, HALF), HALF)

    def d0():
        ref = dbuf.at[own_d, :]
        return remote(ref, ref, d0_s, d0_r, sib)

    def d0_in():
        ref = dbuf.at[pl.ds(pl.multiple_of((x * 2 + 1 - c) * AR, AR), AR), :]
        return remote(ref, ref, d0_s, d0_r, sib)

    def d1(k):
        ref = dbuf.at[drows(r, g), :]
        return remote(ref, ref, d1_s.at[k], d1_r.at[x], (g, lax.rem(x + k, X) * 2 + c, z))

    def xk(k):
        return lax.rem(x + k, X)

    def d1_in(k):
        ref = dbuf.at[drows(xk(k) * 2 + c, g), :]
        return remote(ref, ref, d1_s.at[k], d1_r.at[xk(k)], (g, xk(k) * 2 + c, z))

    def d2(k, j):
        ref = dbuf.at[drows(xk(k) * 2 + c, g), :]
        return remote(ref, ref, d2_s.at[k, j], d2_r.at[xk(k), g], (lax.rem(g + j, G), r, z))

    def d2_in(k, j):
        gg = lax.rem(g + j, G)
        ref = dbuf.at[drows(xk(k) * 2 + c, gg), :]
        return remote(ref, ref, d2_s.at[k, j], d2_r.at[xk(k), gg], (gg, r, z))

    def d3(k, h):
        ref = dbuf.at[drows(xk(k) * 2 + c, h), :]
        return remote(ref, ref, d3_s.at[xk(k), h], d3_r.at[xk(k), h], sib)

    def d3_in(k, h):
        ref = dbuf.at[drows(xk(k) * 2 + 1 - c, h), :]
        return remote(ref, ref, d3_s.at[xk(k), h], d3_r.at[xk(k), h], sib)

    lane_half = lax.broadcasted_iota(jnp.int32, (CH, 128), 1) // 64
    BIG = min(512, T)
    lane_big = lax.broadcasted_iota(jnp.int32, (BIG, 128), 1) // 64

    def big(m):
        return pl.ds(pl.multiple_of(m * BIG, BIG), BIG)

    def rows(m):
        return pl.ds(pl.multiple_of(m * CH, CH), CH)

    low[...] = jnp.zeros_like(low)

    def shrink(rr):
        src = pl.ds(pl.multiple_of(rr * AR, AR), AR)

        @pl.loop(0, T // BIG)
        def _(m):
            y = lax.dot_general(
                tok[big(m), :], dbuf[src, pl.ds(0, F)], (((1,), (1,)), ((), ())),
                preferred_element_type=F32)
            mine = idx_ref[big(m), :] - rr * (AR // 64) - lane_big
            part = low[big(m), :]
            for t in range(AR // 128):
                part += jnp.where(mine == 2 * t, y[:, t * 128:(t + 1) * 128], 0.0)
            low[big(m), :] = part

    cp_tok.wait()
    cp_d.wait()
    cp_u.wait()
    for k in range(1, X):
        d1(k).start()
    d0().start()
    shrink(r)
    cp_w.wait()

    @pl.loop(0, T // BIG)
    def _(m):
        base[big(m), :] = jnp.dot(tok[big(m), :], wbuf[z], preferred_element_type=F32)

    def to_right(b, m):
        return remote(sendbuf.at[b, rows(m), :], from_left.at[b, rows(m), :],
                      rl_s.at[b, m], rl_r.at[b, m], (g, r, lax.rem(z + 1, Z)))

    def to_left(b, m):
        return remote(sendbuf.at[b, rows(m), :], from_right.at[b, rows(m), :],
                      rr_s.at[b, m], rr_r.at[b, m], (g, r, lax.rem(z + Z - 1, Z)))

    def chain_first(b, make):
        @pl.loop(0, M)
        def _(m):
            sendbuf[b, rows(m), :] = jnp.dot(
                tok[rows(m), :], wbuf[b], preferred_element_type=F32).astype(BF16)
            make(b, m).start()

    def chain(b, landed, make):
        @pl.loop(0, M)
        def _(m):
            y = jnp.dot(tok[rows(m), :], wbuf[b], preferred_element_type=F32)
            make(b, m).wait_recv()
            sendbuf[b, rows(m), :] = (y + landed[b, rows(m), :].astype(F32)).astype(BF16)
            make(b, m).start()

    def middle(k):
        right = Z - 1 + z - k

        @pl.when((z > 0) & (right > z) & (right < Z))
        def _():
            chain(right, from_left, to_right)

        left = k - (Z - 1 - z)

        @pl.when((z < Z - 1) & (left >= 0) & (left < z))
        def _():
            chain(left, from_right, to_left)

    def finish_right(b):
        gather_corner(b)
        gather_c(b)

        @pl.when(z == 0)
        def _():
            chain_first(b, to_right)

    def finish_left(b):
        gather_corner(b)
        gather_c(b)

        @pl.when(z == Z - 1)
        def _():
            chain_first(b, to_left)

    blocks(0, gather_a, gather_a)
    for s in range(Z - 1):
        blocks(s, gather_b, gather_b)
        if s + 1 < Z - 1:
            blocks(s + 1, gather_a, gather_a)
        blocks(s, finish_right, finish_left)
        if s == 0:
            for k in range(1, X):
                d1_in(k).wait_recv()
                for j in range(1, G):
                    d2(k, j).start()
                d3(k, g).start()

    d0_in().wait_recv()
    shrink(x * 2 + 1 - c)
    if Z > 2:
        middle(1)
    for k in range(1, X):
        for j in range(1, G):
            d2_in(k, j).wait_recv()
            d3(k, lax.rem(g + j, G)).start()
        shrink(xk(k) * 2 + c)
    for k in range(1, X):
        for h in range(G):
            d3_in(k, h).wait_recv()
        shrink(xk(k) * 2 + 1 - c)

    H = T // 2
    left_lanes = lax.broadcasted_iota(jnp.int32, (H, 128), 1) < 64
    both = low[...]
    both = both + pltpu.roll(both, 64, 1)
    packed = jnp.where(left_lanes, both[:H], both[H:])
    lowin[z] = packed.astype(BF16)

    def lo(k):
        return remote(lowin.at[z], lowin.at[z], lo_s.at[k], lo_r.at[z], (g, r, lax.rem(z + k, Z)))

    def lo_in(k):
        zz = lax.rem(z + k, Z)
        return remote(lowin.at[zz], lowin.at[zz], lo_s.at[k], lo_r.at[zz], (g, r, zz))

    for k in range(1, Z):
        lo(k).start()

    if Z > 2:
        for k in range(2, Z - 1):
            middle(k)

    total = packed
    for k in range(1, Z):
        lo_in(k).wait_recv()
        total = total + lowin[lax.rem(z + k, Z)].astype(F32)
    total = total.astype(BF16).astype(F32)
    other = pltpu.roll(total, 64, 1)
    low[pl.ds(0, H), :] = jnp.where(left_lanes, total, other)
    low[pl.ds(H, H), :] = jnp.where(left_lanes, other, total)

    @pl.loop(0, T // BIG)
    def _(m):
        ss = low[big(m), :]
        who = idx_ref[big(m), :] - lane_big

        def add(rr, acc):
            lhs = jnp.concatenate(
                [jnp.where(who == rr * (AR // 64) + 2 * t, ss, 0.0).astype(BF16) for t in range(AR // 128)],
                axis=1)
            return acc + jnp.dot(
                lhs, dbuf[pl.ds(pl.multiple_of(rr * AR, AR), AR), pl.ds(F, N)],
                preferred_element_type=F32)

        delta = lax.fori_loop(0, R, add, jnp.zeros((BIG, N), F32))
        base[big(m), :] = base[big(m), :] + delta.astype(BF16).astype(F32)

    @pl.when(z > 0)
    def _():
        @pl.loop(0, M)
        def _(m):
            to_right(z, m).wait_recv()
            base[rows(m), :] = base[rows(m), :] + from_left[z, rows(m), :].astype(F32)

    @pl.when(z < Z - 1)
    def _():
        @pl.loop(0, M)
        def _(m):
            to_left(z, m).wait_recv()
            base[rows(m), :] = base[rows(m), :] + from_right[z, rows(m), :].astype(F32)

    out_ref[...] = base[...].astype(BF16)

    for b in range(Z):
        @pl.when(b != z)
        def _(b=b):
            wz(b).wait_send()
            for n in range(LINES):
                wp(b, n).wait_send()
            for i in range(1, X):
                for j in range(1, G):
                    wc(b, i, j, 0).wait_send()
                    wc(b, i, j, 1).wait_send()
            for k in range(C):
                ws(b, k).wait_send()

        @pl.when(b > z)
        def _(b=b):
            @pl.loop(0, M)
            def _(m):
                to_right(b, m).wait_send()

        @pl.when(b < z)
        def _(b=b):
            @pl.loop(0, M)
            def _(m):
                to_left(b, m).wait_send()
    d0().wait_send()
    for k in range(1, X):
        d1(k).wait_send()
        for j in range(1, G):
            d2(k, j).wait_send()
        for h in range(G):
            d3(k, h).wait_send()
    for k in range(1, Z):
        lo(k).wait_send()


def shards(G, R, Z, tokens, token_adapter_index, key_value_weight, adapter_down_weight, adapter_up_weight):
    T, F = tokens.shape
    N = key_value_weight.shape[1]
    A, K, _ = adapter_down_weight.shape
    AR = A * K
    CH = min(256, T)
    M = T // CH
    X = R // 2
    C = G * X
    idx = jnp.broadcast_to(token_adapter_index[:, None], (T, 128))
    dma = pltpu.SemaphoreType.DMA
    any_spec = pl.BlockSpec(memory_space=pl.ANY)
    vmem_spec = pl.BlockSpec(memory_space=pltpu.VMEM)
    return pl.pallas_call(
        functools.partial(kernel, G, R, Z, CH),
        out_shape=jax.ShapeDtypeStruct((T, N), BF16),
        in_specs=[any_spec, vmem_spec, any_spec, any_spec, any_spec],
        out_specs=vmem_spec,
        scratch_shapes=[
            pltpu.VMEM((T, F), BF16),
            pltpu.VMEM((Z, F, N), BF16),
            pltpu.VMEM((R * AR, F + N), BF16),
            pltpu.VMEM((Z, T, N), BF16),
            pltpu.VMEM((Z, T, N), BF16),
            pltpu.VMEM((Z, T, N), BF16),
            pltpu.VMEM((T, 128), F32),
            pltpu.VMEM((Z, T // 2, 128), BF16),
            pltpu.VMEM((T, N), F32),
            dma((4,)), dma((Z,)), dma((Z,)), dma((Z, C)), dma((Z, C)), dma((Z, 2 * C)), dma((Z, 2 * C)), dma((Z, C)), dma((Z, C)),
            dma((Z, M)), dma((Z, M)), dma((Z, M)), dma((Z, M)),
            dma, dma, dma((X,)), dma((X,)), dma((X, G)), dma((X, G)), dma((X, G)), dma((X, G)),
            dma((Z,)), dma((Z,)),
        ],
        compiler_params=pltpu.CompilerParams(
            collective_id=0, has_side_effects=True, vmem_limit_bytes=58 * 1024 * 1024),
    )(tokens, idx, key_value_weight, adapter_down_weight.reshape(AR, F), adapter_up_weight.reshape(AR, N))


def solution(mesh):
    G, R, Z = (mesh.shape[a] for a in ("groups", "replica", "mp"))
    return jax.shard_map(
        functools.partial(shards, G, R, Z),
        mesh=mesh,
        in_specs=(
            P(("groups", "replica"), "mp"),
            P(("groups", "replica")),
            P(None, "mp"),
            P("replica", None, "mp"),
            P("replica", None, "mp"),
        ),
        out_specs=P(("groups", "replica"), "mp"),
        check_vma=False,
    )
```
